128 devices in a mesh: grp: 8 (over z, core), leaf: 16 (over x, y).
Axes of the slice: x: 4, y: 4, z: 4, core: 2. Of those that a mesh axis runs over, the one named last changes fastest.
Arguments:
- points: float32 [524288, 64], P(('grp', 'leaf')), may hold values from -6 to 6
- rhs: float32 [524288, 128], P(('grp', 'leaf')), may hold values from -6 to 6
- leaf_basis: float32 [2048, 256, 128], P(('grp', 'leaf')), may hold values from -0.375 to 0.375
- leaf_skeleton: int32 [2048, 128], P(('grp', 'leaf')), may hold values from 0 to 255, as said below
- node_basis: float32 [128, 2048, 128], P(('grp', 'leaf')), may hold values from -0.125 to 0.125
- node_skeleton: int32 [128, 128], P(('grp', 'leaf')), may hold values from 0 to 2047, as said below
- group_basis: float32 [8, 2048, 128], P('grp', 'leaf'), may hold values from -0.125 to 0.125
- group_skeleton: int32 [8, 128], P('grp'), may hold values from 0 to 2047, as said below
- near_live: int32 [2048, 9], P(('grp', 'leaf')), may hold values from 0 to 1, as said below
Outputs:
- product: float32 [524288, 128], P(('grp', 'leaf'))
The draws below stay inside these ranges and needn't reach their ends.
Inputs may be any that keep to these rules, and one draw needn't show every extreme that they name: `leaf_skeleton`: the indices of one row are distinct. `node_skeleton`: the indices of one row are distinct. `group_skeleton`: the indices of one row are distinct. `near_live`: column 4 is 1 everywhere; entries whose leaf lies outside the row's coarse node are 0; the share of live tiles differs from device to device.
All inputs are finite; a program needn't handle non-finite values.
Results may differ from the reference program's by a relative error of at most 0.0003.
Values sent between devices are 32-bit elements; how exact they have to be, the bound alone decides.
A program may use at most 128 MiB of HBM per device.

```python
import jax
import jax.numpy as jnp
from jax import lax

D = 64
NRHS = 128
LEAF = 256
RANK = 128
NEAR = 4
LD = 16
LEAVES = 2048
NODES = 128
NPOINTS = 524288
N_GRP = 8
N_LEAF = 16


def distinct_rows(key, total_rows, pool_size, kept_count):
    scores = jax.random.randint(key, (total_rows, pool_size), 0, 4096) * pool_size + jnp.arange(pool_size, dtype=jnp.int32)[None, :]
    ranking = jnp.argsort(scores, axis=1, stable=True)
    return ranking[:, :kept_count].astype(jnp.int32)


def draw_leaf_skeleton(key, part):
    key = jax.random.fold_in(key, 11)
    return distinct_rows(key, LEAVES, LEAF, RANK)


def draw_node_skeleton(key, part):
    key = jax.random.fold_in(key, 13)
    return distinct_rows(key, NODES, LD * RANK, RANK)


def draw_group_skeleton(key, part):
    key = jax.random.fold_in(key, 17)
    return distinct_rows(key, N_GRP, N_LEAF * RANK, RANK)


def draw_near_live(key, part):
    key = jax.random.fold_in(key, 19)
    key_rate, key_roll = jax.random.split(key)
    window = 2 * NEAR + 1
    thresholds = jax.random.randint(key_rate, (NODES,), 30, 96)
    dice_rolls = jax.random.randint(key_roll, (LEAVES, window), 0, 100)
    leaf_ids = jnp.arange(LEAVES, dtype=jnp.int32)[:, None]
    offsets = jnp.arange(window, dtype=jnp.int32)[None, :] - NEAR
    position = leaf_ids % (N_LEAF * LD) + offsets
    inside = (position >= 0) & (position < N_LEAF * LD)
    alive_mask = (dice_rolls < thresholds[leaf_ids // LD]) | (offsets == 0)
    return (alive_mask & inside).astype(jnp.int32)


def block_levels(rng, extent, cuts, least, top_value):
    def one(dim, blocks):
        heights = jax.random.uniform(jax.random.fold_in(jax.random.fold_in(rng, 6), dim), (blocks,), jnp.float32, least / len(cuts), top_value / len(cuts))
        return jnp.repeat(jnp.exp(heights), extent[dim] // blocks).reshape((-1,) + (1,) * (len(extent) - dim - 1))

    level = one(*cuts[0])
    for cut in cuts[1:]:
        level = level * one(*cut)
    return level


def scatter_about(rng, dims, deviation, reach, pieces=(), kind=jnp.bfloat16):
    entries = deviation * jax.random.normal(rng, dims, jnp.float32)
    if pieces:
        entries = entries * block_levels(rng, dims, pieces, -0.22, 0.18)
    return jnp.clip(entries, -reach, reach).astype(kind)


def setup_inputs(seed: int = 0) -> dict:
    key_of = jax.random.split(jax.random.key(seed), 10)
    return {
        "points": scatter_about(key_of[0], (NPOINTS, D), 1.0, 6.0, ((0, 128),), jnp.float32),
        "rhs": scatter_about(key_of[1], (NPOINTS, NRHS), 1.0, 6.0, ((0, 128),), jnp.float32),
        "leaf_basis": scatter_about(key_of[2], (LEAVES, LEAF, RANK), LEAF ** -0.5, 0.375, ((0, 128),), jnp.float32),
        "leaf_skeleton": draw_leaf_skeleton(jax.random.fold_in(key_of[9], 71), 0),
        "node_basis": scatter_about(key_of[4], (NODES, LD * RANK, RANK), (LD * RANK) ** -0.5, 0.125, ((0, 128),), jnp.float32),
        "node_skeleton": draw_node_skeleton(jax.random.fold_in(key_of[9], 71), 0),
        "group_basis": scatter_about(key_of[6], (N_GRP, N_LEAF * RANK, RANK), (N_LEAF * RANK) ** -0.5, 0.125, ((0, 8), (1, 16)), jnp.float32),
        "group_skeleton": draw_group_skeleton(jax.random.fold_in(key_of[9], 71), 0),
        "near_live": draw_near_live(jax.random.fold_in(key_of[9], 71), 0),
    }


highest = lax.Precision.HIGHEST


def kernel(left_pts, right_pts):
    distance = jnp.sum(left_pts * left_pts, axis=1)[:, None] + jnp.sum(right_pts * right_pts, axis=1)[None, :] - 2.0 * jnp.dot(left_pts, right_pts.T, precision=highest)
    return jnp.exp(distance * (-2.0 / left_pts.shape[1]))


def pick(source_table, indices):
    return source_table[indices]


def reference(points, rhs, leaf_basis, leaf_skeleton, node_basis, node_skeleton, group_basis, group_skeleton, near_live):
    group_leaves = N_LEAF * LD
    window = 2 * NEAR + 1
    leaf_points = points.reshape(LEAVES, LEAF, D)
    leaf_rhs = rhs.reshape(LEAVES, LEAF, NRHS)
    leaf_coef = jnp.einsum("lpr,lpc->lrc", leaf_basis, leaf_rhs, precision=highest)
    node_coef = jnp.einsum("akr,akc->arc", node_basis, leaf_coef.reshape(NODES, LD * RANK, NRHS), precision=highest)
    group_coef = jnp.einsum("gkr,gkc->grc", group_basis, node_coef.reshape(N_GRP, N_LEAF * RANK, NRHS), precision=highest)
    leaf_pts = jax.vmap(pick)(leaf_points, leaf_skeleton)
    node_pts = jax.vmap(pick)(leaf_pts.reshape(NODES, LD * RANK, D), node_skeleton)
    group_pts = jax.vmap(pick)(node_pts.reshape(N_GRP, N_LEAF * RANK, D), group_skeleton)
    group_ids = jnp.arange(N_GRP, dtype=jnp.int32)

    def coarse(group_id):
        blocks = jax.vmap(kernel, (None, 0))(group_pts[group_id], group_pts)
        weights = (group_ids != group_id).astype(jnp.float32)
        return jnp.einsum("g,grs,gsc->rc", weights, blocks, group_coef, precision=highest)

    group_field = lax.map(coarse, group_ids)
    grouped_pts = node_pts.reshape(N_GRP, N_LEAF, RANK, D)
    grouped_coef = node_coef.reshape(N_GRP, N_LEAF, RANK, NRHS)
    group_slabs = group_basis.reshape(N_GRP, N_LEAF, RANK, RANK)
    leaf_ids = jnp.arange(N_LEAF, dtype=jnp.int32)

    def middle(node_id):
        group_id = node_id // N_LEAF
        position = node_id % N_LEAF
        blocks = jax.vmap(kernel, (None, 0))(node_pts[node_id], grouped_pts[group_id])
        weights = (jnp.abs(leaf_ids - position) >= 2).astype(jnp.float32)
        far_field = jnp.einsum("k,krs,ksc->rc", weights, blocks, grouped_coef[group_id], precision=highest)
        return far_field + jnp.dot(group_slabs[group_id, position], group_field[group_id], precision=highest)

    node_field = lax.map(middle, jnp.arange(NODES, dtype=jnp.int32))
    leaf_field = jnp.einsum("akr,arc->akc", node_basis, node_field, precision=highest).reshape(LEAVES, RANK, NRHS)
    far_out = jnp.einsum("lpr,lrc->lpc", leaf_basis, leaf_field, precision=highest)
    packed = jnp.concatenate([points, rhs], axis=1).reshape(N_GRP, group_leaves * LEAF, D + NRHS)
    padded = jnp.pad(packed, ((0, 0), (NEAR * LEAF, NEAR * LEAF), (0, 0)))
    anchor = jnp.zeros((), jnp.int32)

    def near_leaf(leaf_id):
        group_id = leaf_id // group_leaves
        position = leaf_id % group_leaves
        window_rows = lax.dynamic_slice(padded, (group_id, position * LEAF, anchor), (1, window * LEAF, D + NRHS))[0]
        column_mask = jnp.repeat(near_live[leaf_id].astype(jnp.float32), LEAF)
        kernel_block = kernel(leaf_points[leaf_id], window_rows[:, :D]) * column_mask[None, :]
        return jnp.dot(kernel_block, window_rows[:, D:], precision=highest)

    near_out = lax.map(near_leaf, jnp.arange(LEAVES, dtype=jnp.int32))
    return (near_out + far_out).reshape(NPOINTS, NRHS)
```

```python
import functools
import math

import jax
import jax.numpy as jnp
from jax import lax
from jax.experimental import pallas as pl
from jax.experimental.pallas import tpu as pltpu
from jax.sharding import PartitionSpec as P

MESH = pl.DeviceIdType.MESH
f32 = jnp.float32
bf16 = jnp.bfloat16
NT = (((1,), (1,)), ((), ()))
TN = (((0,), (0,)), ((), ()))

D = 64
NRHS = 128
LEAF = 256
RANK = 128
NEAR = 4
LD = 16
ROWS = LD * LEAF
N_GRP = 8
N_LEAF = 16
SIDE = 4
ALPHA = math.sqrt(4.0 / D * math.log2(math.e))
DEAD = -32768.0
NORM_U, NORM_V, MASK = 64, 67, 70


def dot(a, b):
    return jnp.dot(a, b, preferred_element_type=f32)


def split(x):
    high = x.astype(bf16)
    return high, (x - high.astype(f32)).astype(bf16)


def halves(x):
    return x[:, :128] + x[:, 128:]


def mm3(a, b):
    a_high, a_low = split(a)
    b_high, b_low = split(b)
    row = jnp.concatenate([b_high, b_low], axis=1)
    return halves(dot(jnp.concatenate([a_high, a_low], axis=1), jnp.concatenate([row, row], axis=0)))


def lanes(shape):
    return lax.broadcasted_iota(jnp.int32, shape, 1)


def twice(packed):
    low = lanes(packed.shape) < D
    other = pltpu.roll(packed, D, 1)
    return jnp.concatenate([jnp.where(low, packed, other), jnp.where(low, other, packed)], axis=0)


def pack(doubled):
    half = doubled.shape[0] // 2
    top = doubled[:half]
    return jnp.where(lanes(top.shape) < D, top, doubled[half:])


def base_u():
    lane = lanes((1, 128))
    return ((lane >= NORM_V) & (lane < NORM_V + 3)).astype(f32)


def base_v():
    lane = lanes((1, 128))
    return ((lane >= NORM_U) & (lane < NORM_U + 3)).astype(f32)


def features(doubled, u_row, v_row):
    scaled = doubled * ALPHA
    high = scaled.astype(bf16).astype(f32)
    low = (scaled - high).astype(bf16).astype(f32)
    both = high + low
    norm = -0.25 * jnp.sum(both * both, axis=1, keepdims=True)
    n1 = norm.astype(bf16).astype(f32)
    n2 = (norm - n1).astype(bf16).astype(f32)
    n3 = norm - n1 - n2
    lane = lanes(doubled.shape)
    first = lane < D
    u = v = None
    if u_row is not None:
        extra = jnp.where(lane == NORM_U, n1, jnp.where(lane == NORM_U + 1, n2, jnp.where(lane == NORM_U + 2, n3, u_row)))
        u = jnp.concatenate([jnp.where(first, high, low), jnp.where(first, high, extra)], axis=1).astype(bf16)
    if v_row is not None:
        extra = jnp.where(lane == NORM_V, n1, jnp.where(lane == NORM_V + 1, n2, jnp.where(lane == NORM_V + 2, n3, v_row)))
        v = jnp.concatenate([high, jnp.where(first, low, extra)], axis=1).astype(bf16)
    return u, v


def kernel_block(u, v):
    return split(jnp.exp2(lax.dot_general(u, v, NT, preferred_element_type=f32)))


def apply_block(k_high, k_low, r):
    return halves(dot(k_high, r)) + dot(k_low, r[:, :128])


def body(
    points, rhs, leaf_basis, node_basis, group_basis, leaf_skel, node_skel, group_skel, live,
    out,
    pts, rh, lb, nb, gb, U, V, R, WW, acc, bias, wr, pk,
    npts, npk, gpart, gsum, gfull, gpk, gall, gct, ctp, gcs, gc, ft, fmine,
    halo_p, halo_r, src_p, tgt_p, src_c, part, fr, coef,
    in_sem, out_sem, hs_p, hr_p, hs_r, hr_r, xs_p, xr_p, ys_p, yr_p, xs_c, xr_c, ys_f, yr_f,
    s1, r1, s2, r2, s3, r3, s4, r4, s5, r5, s6, r6,
):
    g = lax.axis_index("grp")
    l = lax.axis_index("leaf")
    x = l // SIDE
    y = lax.rem(l, SIDE)

    def leaf_peer(k):
        return lax.rem(l + k, N_LEAF)

    def grp_peer(k):
        return lax.rem(g + k, N_GRP)

    def x_peer(k):
        return lax.rem(x + k, SIDE) * SIDE + y

    def y_peer(k):
        return x * SIDE + lax.rem(y + k, SIDE)

    barrier = pltpu.get_barrier_semaphore()
    for k in range(1, N_LEAF):
        pl.semaphore_signal(barrier, inc=1, device_id=(g, leaf_peer(k)), device_id_type=MESH)
    for k in range(1, N_GRP):
        pl.semaphore_signal(barrier, inc=1, device_id=(grp_peer(k), l), device_id_type=MESH)

    loads = [
        pltpu.make_async_copy(src, dst, in_sem.at[i])
        for i, (src, dst) in enumerate(
            ((points, pts), (rhs, rh), (node_basis, nb), (leaf_basis, lb), (group_basis, gb))
        )
    ]
    for load in loads:
        load.start()

    row_id = lax.broadcasted_iota(jnp.int32, (LD, 128), 0)
    column = lax.broadcasted_iota(jnp.int32, (LD, 128), 1)
    table = jnp.zeros((LD, 128), f32)
    alive = live[...].astype(f32)
    for j in range(2 * NEAR + 1):
        dead = (1.0 - alive[:, j : j + 1]) * DEAD
        table = jnp.where(column == row_id + (MASK + j), dead, table)
    bias[...] = table + base_u()

    def one_hot(s):
        return base_v() + (lanes((1, 128)) == MASK + s).astype(f32)

    def own_features(t):
        rows = pl.ds(pl.multiple_of(t * LEAF, LEAF), LEAF)
        value = pts[rows, :]
        doubled = jnp.concatenate([value, value], axis=1)
        u, v = features(doubled, bias[pl.ds(t, 1), :], one_hot(t + NEAR))
        U[rows, :] = u
        V[pl.ds(pl.multiple_of((t + NEAR) * LEAF, LEAF), LEAF), :] = v
        return doubled

    loads[0].wait()

    def edge(i, carry):
        t = jnp.where(i < NEAR, i, i + LD - 2 * NEAR)
        pk[i] = pack(own_features(t))
        return carry

    lax.fori_loop(0, 2 * NEAR, edge, 0)

    def pick(r, carry):
        index = node_skel[0, r]
        leaf = index // RANK
        row = leaf * LEAF + leaf_skel[leaf, lax.rem(index, RANK)]
        npts[pl.ds(r, 1), :] = pts[pl.ds(row, 1), :]
        return carry

    lax.fori_loop(0, RANK, pick, 0, unroll=8)
    value = npts[...]
    npk[...] = pack(jnp.concatenate([value, value], axis=1))

    def pick_group(r, carry):
        index = group_skel[0, r]
        inside = (index // RANK == l).astype(f32)
        gpart[pl.ds(r, 1), :] = npts[pl.ds(lax.rem(index, RANK), 1), :] * inside
        return carry

    lax.fori_loop(0, RANK, pick_group, 0, unroll=8)
    value = gpart[...]
    gsum[...] = jnp.concatenate([value, value], axis=1)

    pl.semaphore_wait(barrier, N_LEAF + N_GRP - 2)

    sends = []

    def send(src, dst, send_sem, recv_sem, device):
        copy = pltpu.make_async_remote_copy(
            src_ref=src, dst_ref=dst, send_sem=send_sem, recv_sem=recv_sem, device_id=device, device_id_type=MESH
        )
        copy.start()
        sends.append(copy)
        return copy

    def to_leaf(src_of, dst_of, send_sem, recv_sem):
        return [
            send(src_of(leaf_peer(k)), dst_of(k), send_sem.at[k - 1], recv_sem.at[k - 1], (g, leaf_peer(k)))
            for k in range(1, N_LEAF)
        ]

    def to_grp(src, dst, send_sem, recv_sem):
        return [
            send(src, dst, send_sem.at[k - 1], recv_sem.at[k - 1], (grp_peer(k), l)) for k in range(1, N_GRP)
        ]

    def to_x(src, dst, send_sem, recv_sem):
        return [send(src, dst, send_sem.at[k - 1], recv_sem.at[k - 1], (g, x_peer(k))) for k in range(1, SIDE)]

    def eight(i):
        return pl.ds(pl.multiple_of(i * 8, 8), 8)

    sum_pts = to_leaf(lambda p: gsum.at[eight(p)], lambda k: gct.at[k - 1], s1, r1)
    x_pts = to_x(npk, src_p.at[x], xs_p, xr_p)
    y_pts = [
        send(npk, tgt_p.at[y], ys_p.at[k - 1], yr_p.at[k - 1], (g, y_peer(k))) for k in range(1, SIDE)
    ]
    src_p[x] = npk[...]
    tgt_p[y] = npk[...]
    halo = {}
    for c in range(NEAR):
        for side, (slot, leaf, device) in enumerate(
            ((2 * NEAR - 1 - c, LD - 1 - c, leaf_peer(1)), (c, c, leaf_peer(N_LEAF - 1)))
        ):
            halo[side, c] = (
                send(pk.at[slot], halo_p.at[side, c], hs_p.at[side, c], hr_p.at[side, c], (g, device)),
                send(
                    rhs.at[pl.ds(leaf * LEAF, LEAF)], halo_r.at[side, c], hs_r.at[side, c], hr_r.at[side, c], (g, device)
                ),
            )

    loads[1].wait()
    loads[2].wait()
    loads[3].wait()
    loads[4].wait()
    wr[...] = jnp.zeros((256, 256), f32)

    def up(t, carry):
        rows = pl.ds(pl.multiple_of(t * LEAF, LEAF), LEAF)
        r_high, r_low = split(rh[rows, :])
        r = jnp.concatenate([r_high, r_low], axis=1)
        R[pl.ds(pl.multiple_of((t + NEAR) * LEAF, LEAF), LEAF), :] = r
        w = mm3(lb[rows, :], nb[pl.ds(pl.multiple_of(t * RANK, RANK), RANK), :])
        w_high, w_low = split(w)
        w = jnp.concatenate([w_high, w_low], axis=1)
        WW[rows, :] = w
        wr[...] += lax.dot_general(w, r, TN, preferred_element_type=f32)
        return carry

    lax.fori_loop(0, LD, up, 0)
    node_coef = halves(wr[0:128, :] + wr[128:256, :])
    coef[...] = node_coef
    x_coef = to_x(coef, src_c.at[x], xs_c, xr_c)
    src_c[x] = node_coef
    ctp[...] = mm3(node_coef.T, gb[...])
    sum_coef = to_leaf(lambda p: ctp.at[eight(p)], lambda k: gcs.at[k - 1], s2, r2)

    def middle(t, carry):
        own_features(t)
        return carry

    lax.fori_loop(NEAR, LD - NEAR, middle, 0)

    def tiles(t, count, s):
        rows = pl.ds(pl.multiple_of(t * LEAF, LEAF), count * LEAF)
        source = pl.ds(pl.multiple_of((s + NEAR) * LEAF, LEAF), LEAF)
        k_high, k_low = kernel_block(U[rows, :], V[source, :])
        acc[rows, :] += apply_block(k_high, k_low, R[source, :])

    def full(i, carry):
        b = i // 6
        tiles(b * 4, 4, b * 4 - 1 + lax.rem(i, 6))
        return carry

    def left(b):
        for c in range(1, NEAR):
            tiles(b * 4, NEAR - c, b * 4 - 1 - c)

    def right(b):
        for c in range(1, NEAR):
            tiles(b * 4 + c, NEAR - c, b * 4 + 4 + c)

    def partial(j, carry):
        left(j + 1)
        right(j)
        return carry

    acc[...] = jnp.zeros((ROWS, NRHS), f32)
    lax.fori_loop(1, 4, full, 0)

    for copy in sum_pts:
        copy.wait_recv()
    total = gsum[eight(l), :]
    for k in range(N_LEAF - 1):
        total = total + gct[k]
    gpart8 = eight(l)
    gfull[gpart8, :] = total
    full_pts = to_leaf(lambda p: gfull.at[gpart8], lambda k: gfull.at[gpart8], s3, r3)

    lax.fori_loop(4, 7, full, 0)

    for copy in sum_coef:
        copy.wait_recv()
    total = ctp[eight(l), :]
    for k in range(N_LEAF - 1):
        total = total + gcs[k]
    fmine[0] = total
    gc_out = to_grp(fmine.at[0], gc.at[g], s4, r4)
    gc[g] = jnp.zeros((8, 128), f32)
    for copy in full_pts:
        copy.wait_recv()
    gpk[...] = pack(gfull[...])
    all_pts = to_grp(gpk, gall.at[g], s5, r5)
    gall[g] = gpk[...]

    for copy in x_pts + y_pts + x_coef:
        copy.wait_recv()
    lane = lanes((1, 128))
    us, vs, rs = [], [], []
    for i in range(SIDE):
        u_row = base_u()
        for j in range(SIDE):
            close = jnp.abs(SIDE * x + i - SIDE * j - y) < 2
            u_row = u_row + jnp.where(lane == MASK + j, jnp.where(close, DEAD, 0.0), 0.0)
        us.append(features(twice(tgt_p[i]), u_row, None)[0])
        vs.append(features(twice(src_p[i]), None, one_hot(i))[1])
        rs.append(jnp.concatenate(split(src_c[i]), axis=1))
    k_high, k_low = kernel_block(jnp.concatenate(us, axis=0), jnp.concatenate(vs, axis=0))
    field = apply_block(k_high, k_low, jnp.concatenate(rs, axis=0))
    for i in range(SIDE):
        part[i] = field[i * 128 : (i + 1) * 128]
    y_field = [
        send(part.at[lax.rem(y + k, SIDE)], fr.at[k - 1], ys_f.at[k - 1], yr_f.at[k - 1], (g, y_peer(k)))
        for k in range(1, SIDE)
    ]

    lax.fori_loop(7, 13, full, 0)

    for copy in gc_out + all_pts:
        copy.wait_recv()
    u_own = features(twice(gpk[...]), base_u(), None)[0]
    v_all = jnp.concatenate([features(twice(gall[h]), None, base_v())[1] for h in range(N_GRP)], axis=0)
    k_high, k_low = kernel_block(v_all, u_own)
    columns = jnp.concatenate([gc[h] for h in range(N_GRP)], axis=1)
    c_high = columns.astype(bf16)
    c_low = (columns - c_high.astype(f32)).astype(bf16)
    mine = halves(
        dot(c_high, jnp.concatenate([k_high, k_low], axis=1)) + dot(c_low, jnp.concatenate([k_high, k_low], axis=1))
    )
    ft[eight(l), :] = mine
    field_out = to_leaf(lambda p: ft.at[eight(l)], lambda k: ft.at[eight(l)], s6, r6)

    lax.fori_loop(13, 23, full, 0)
    lax.fori_loop(0, 3, partial, 0)

    for c in range(NEAR):
        for side in range(2):
            for copy in halo[side, c]:
                copy.wait_recv()
            s = -1 - c if side == 0 else LD + c
            where = pl.ds((s + NEAR) * LEAF, LEAF)
            V[where, :] = features(twice(halo_p[side, c]), None, one_hot(s + NEAR))[1]
            R[where, :] = jnp.concatenate(split(halo_r[side, c]), axis=1)
            tiles(0 if side == 0 else LD - NEAR + c, NEAR - c, s)

    for copy in y_field + field_out:
        copy.wait_recv()
    node_field = part[y] + fr[0] + fr[1] + fr[2] + mm3(gb[...], ft[...].T)
    row = jnp.concatenate(split(node_field), axis=1)
    both = jnp.concatenate([row, row], axis=0)
    stores = []
    for i in range(4):
        rows = pl.ds(i * 1024, 1024)
        acc[rows, :] += halves(dot(WW[rows, :], both))
        store = pltpu.make_async_copy(acc.at[rows], out.at[rows], out_sem.at[i])
        store.start()
        stores.append(store)
    for copy in sends:
        copy.wait_send()
    for store in stores:
        store.wait()


def per_device(
    points, rhs, leaf_basis, leaf_skeleton, node_basis, node_skeleton, group_basis, group_skeleton, near_live
):
    any_ = pl.BlockSpec(memory_space=pl.ANY)
    smem = pl.BlockSpec(memory_space=pltpu.SMEM)
    vmem = pl.BlockSpec(memory_space=pltpu.VMEM)
    dma = pltpu.SemaphoreType.DMA
    V = pltpu.VMEM
    scratch = [
        V((ROWS, D), f32), V((ROWS, NRHS), f32), V((ROWS, RANK), f32), V((LD * RANK, RANK), f32), V((RANK, RANK), f32),
        V((ROWS, 256), bf16), V((ROWS + 2 * NEAR * LEAF, 256), bf16), V((ROWS + 2 * NEAR * LEAF, 256), bf16),
        V((ROWS, 256), bf16), V((ROWS, NRHS), f32), V((LD, 128), f32), V((256, 256), f32), V((2 * NEAR, 128, 128), f32),
        V((RANK, D), f32), V((64, 128), f32), V((RANK, D), f32), V((RANK, 128), f32), V((RANK, 128), f32),
        V((64, 128), f32), V((N_GRP, 64, 128), f32), V((N_LEAF - 1, 8, 128), f32), V((128, 128), f32),
        V((N_LEAF - 1, 8, 128), f32), V((N_GRP, 8, 128), f32), V((128, 128), f32), V((1, 8, 128), f32),
        V((2, NEAR, 128, 128), f32), V((2, NEAR, LEAF, 128), f32), V((SIDE, 64, 128), f32), V((SIDE, 64, 128), f32),
        V((SIDE, 128, 128), f32), V((SIDE, 128, 128), f32), V((SIDE - 1, 128, 128), f32), V((128, 128), f32),
        dma((5,)), dma((4,)), dma((2, NEAR)), dma((2, NEAR)), dma((2, NEAR)), dma((2, NEAR)),
        dma((3,)), dma((3,)), dma((3,)), dma((3,)), dma((3,)), dma((3,)), dma((3,)), dma((3,)),
        dma((15,)), dma((15,)), dma((15,)), dma((15,)), dma((15,)), dma((15,)),
        dma((7,)), dma((7,)), dma((7,)), dma((7,)), dma((15,)), dma((15,)),
    ]
    return pl.pallas_call(
        body,
        out_shape=jax.ShapeDtypeStruct((ROWS, NRHS), f32),
        in_specs=[any_, any_, any_, any_, any_, smem, smem, smem, vmem],
        out_specs=any_,
        scratch_shapes=scratch,
        compiler_params=pltpu.CompilerParams(
            collective_id=0, has_side_effects=True, vmem_limit_bytes=56 * 1024 * 1024
        ),
    )(
        points, rhs, leaf_basis.reshape(ROWS, RANK), node_basis.reshape(LD * RANK, RANK), group_basis.reshape(RANK, RANK),
        leaf_skeleton, node_skeleton, group_skeleton, near_live,
    )


def solution(mesh):
    return jax.shard_map(
        per_device,
        mesh=mesh,
        in_specs=(
            P(("grp", "leaf"), None),
            P(("grp", "leaf"), None),
            P(("grp", "leaf"), None, None),
            P(("grp", "leaf"), None),
            P(("grp", "leaf"), None, None),
            P(("grp", "leaf"), None),
            P("grp", "leaf", None),
            P("grp", None),
            P(("grp", "leaf"), None),
        ),
        out_specs=P(("grp", "leaf"), None),
        check_vma=False,
    )
```

```python
import functools
import math

import jax
import jax.numpy as jnp
from jax import lax
from jax.experimental import pallas as pl
from jax.experimental.pallas import tpu as pltpu
from jax.sharding import PartitionSpec as P

MESH = pl.DeviceIdType.MESH
f32 = jnp.float32
bf16 = jnp.bfloat16
NT = (((1,), (1,)), ((), ()))

D = 64
NRHS = 128
LEAF = 256
RANK = 128
NEAR = 4
LD = 16
ROWS = LD * LEAF
N_GRP = 8
N_LEAF = 16
SIDE = 4
ALPHA = math.sqrt(4.0 / D * math.log2(math.e))
DEAD = -32768.0
MASK = 8
PAD = NEAR * LEAF


def dot(a, b):
    return jnp.dot(a, b, preferred_element_type=f32)


def split(x):
    high = x.astype(bf16)
    return high, (x - high.astype(f32)).astype(bf16)


def pieces(x):
    high = x.astype(bf16)
    rest = x - high.astype(f32)
    middle = rest.astype(bf16)
    return jnp.concatenate([high, middle, (rest - middle.astype(f32)).astype(bf16)], axis=0)


def thirds(x):
    n = x.shape[0] // 3
    return x[:n] + x[n : 2 * n] + x[2 * n :]


def halves(x):
    return x[:, :128] + x[:, 128:]


def mm3(a, b):
    a_high, a_low = split(a)
    b_high, b_low = split(b)
    row = jnp.concatenate([b_high, b_low], axis=1)
    return halves(dot(jnp.concatenate([a_high, a_low], axis=1), jnp.concatenate([row, row], axis=0)))


def rows_of(shape):
    return lax.broadcasted_iota(jnp.int32, shape, 0)


def base_u():
    row = rows_of((D, 1))
    return ((row >= 3) & (row < 6)).astype(f32)


def base_v():
    return (rows_of((D, 1)) < 3).astype(f32)


def one_hot(s):
    return base_v() + (rows_of((D, 1)) == MASK + s).astype(f32)


def features(coordinates, u_col, v_col):
    n = coordinates.shape[1]
    scaled = coordinates * ALPHA
    high = scaled.astype(bf16)
    low = (scaled - high.astype(f32)).astype(bf16)
    both = high.astype(f32) + low.astype(f32)
    norm = -0.5 * jnp.sum(both * both, axis=0, keepdims=True)
    n1 = norm.astype(bf16).astype(f32)
    n2 = (norm - n1).astype(bf16).astype(f32)
    n3 = norm - n1 - n2
    row = rows_of((8, n))
    result = []
    for first, col, blocks in ((0, u_col, (high, low, high)), (3, v_col, (high, high, low))):
        if col is None:
            result.append(None)
            continue
        top = jnp.where(
            row == first, n1, jnp.where(row == first + 1, n2, jnp.where(row == first + 2, n3, col[:8]))
        )
        extra = jnp.concatenate([top, jnp.broadcast_to(col[8:], (D - 8, n))], axis=0).astype(bf16)
        result.append(jnp.concatenate([*blocks, extra], axis=0))
    return result


def flip(x, eye):
    return lax.dot_general(eye, x, NT, preferred_element_type=f32).astype(bf16)


def kernel_block(u, v):
    return split(jnp.exp2(dot(u, v)))


def apply_block(k_high, k_low, r):
    return halves(dot(k_high, r)) + dot(k_low, r[:, :128])


def mask_table(alive, shift):
    shape = (D, 128)
    row = rows_of(shape)
    leaf = lax.broadcasted_iota(jnp.int32, shape, 1)
    table = jnp.where((row >= MASK) & (row < MASK + LD + 2 * NEAR), DEAD, 0.0)
    for j in range(2 * NEAR + 1):
        here = (row == leaf + (MASK + j + shift)) & (row >= MASK)
        table = jnp.where(here, (1.0 - alive[j : j + 1, :]) * DEAD, table)
    return table + base_u()


def column(table, t):
    lane = lax.broadcasted_iota(jnp.int32, table.shape, 1)
    return jnp.sum(jnp.where(lane == t, table, 0.0), axis=1, keepdims=True)


def body(
    points, rhs, leaf_basis, node_basis, group_basis, leaf_skel, node_skel, group_skel, live,
    out,
    pts, rh, lb, nb, gb, U, VT, R, WW, acc, bias, wr, lt, flat,
    px, ty, gpy, py, gall, coef, src_c, ctp, gcs, gc, fmine, ft, part, fr,
    hp, hl, hr, UH, accH, hpart,
    in_sem, out_sem, xs1, xr1, ys1, yr1, ys2, yr2, xs3, xr3, ys4, yr4,
    gs1, gr1, gs2, gr2, s1, r1, s2, r2, hs1, hr1, hs2, hr2, hs3, hr3, hs4, hr4,
):
    g = lax.axis_index("grp")
    l = lax.axis_index("leaf")
    x = l // SIDE
    y = lax.rem(l, SIDE)

    def leaf_peer(k):
        return lax.rem(l + k, N_LEAF)

    def grp_peer(k):
        return lax.rem(g + k, N_GRP)

    def x_peer(k):
        return lax.rem(x + k, SIDE) * SIDE + y

    def y_peer(k):
        return x * SIDE + lax.rem(y + k, SIDE)

    barrier = pltpu.get_barrier_semaphore()
    for k in range(1, N_LEAF):
        pl.semaphore_signal(barrier, inc=1, device_id=(g, leaf_peer(k)), device_id_type=MESH)
    for k in range(1, N_GRP):
        pl.semaphore_signal(barrier, inc=1, device_id=(grp_peer(k), l), device_id_type=MESH)

    loads = [
        pltpu.make_async_copy(src, dst, in_sem.at[i])
        for i, (src, dst) in enumerate(
            ((points, pts), (rhs, rh), (node_basis, nb), (leaf_basis, lb), (group_basis, gb))
        )
    ]
    for load in loads:
        load.start()

    flat[...] = jnp.zeros((128, 128), f32)
    flat[0:LD, 0 : 2 * NEAR + 1] = live[...].astype(f32)
    alive = flat[...].T[0:16]
    lt[...] = alive
    bias[0] = mask_table(alive, 0)

    skeleton = node_skel[...]
    leaf = skeleton // RANK
    place = lax.rem(skeleton, RANK)
    hot = (rows_of((RANK, RANK)) == place).astype(bf16)
    table = dot(leaf_skel[...].astype(f32).astype(bf16), hot)
    within = jnp.sum(jnp.where(rows_of((LD, RANK)) == leaf, table, 0.0), axis=0, keepdims=True)
    target = leaf.astype(f32) * LEAF + within
    row256 = rows_of((LEAF, RANK)).astype(f32)
    loads[0].wait()

    def pick(t, total):
        hot = (row256 == target - t.astype(f32) * LEAF).astype(bf16)
        cols = pl.ds(pl.multiple_of(t * LEAF, LEAF), LEAF)
        return total + dot(pieces(pts[:, cols]), hot)

    node_pts = thirds(lax.fori_loop(0, LD, pick, jnp.zeros((3 * D, RANK), f32)))
    hot = (rows_of((RANK, RANK)) + l * RANK == group_skel[...]).astype(bf16)
    px[x, 0:D, :] = node_pts
    px[x, D : 2 * D, :] = thirds(dot(pieces(node_pts), hot))
    ty[y] = node_pts

    pl.semaphore_wait(barrier, N_LEAF + N_GRP - 2)

    sends = []

    def send(src, dst, send_sem, recv_sem, device):
        copy = pltpu.make_async_remote_copy(
            src_ref=src, dst_ref=dst, send_sem=send_sem, recv_sem=recv_sem, device_id=device, device_id_type=MESH
        )
        copy.start()
        sends.append(copy)
        return copy

    def to_leaf(src_of, dst_of, send_sem, recv_sem):
        return [
            send(src_of(leaf_peer(k)), dst_of(k), send_sem.at[k - 1], recv_sem.at[k - 1], (g, leaf_peer(k)))
            for k in range(1, N_LEAF)
        ]

    def to_grp(src, dst, send_sem, recv_sem):
        return [
            send(src, dst, send_sem.at[k - 1], recv_sem.at[k - 1], (grp_peer(k), l)) for k in range(1, N_GRP)
        ]

    def to_x(src, dst, send_sem, recv_sem):
        return [send(src, dst, send_sem.at[k - 1], recv_sem.at[k - 1], (g, x_peer(k))) for k in range(1, SIDE)]

    def to_y(src_of, dst_of, send_sem, recv_sem):
        return [
            send(src_of(k), dst_of(k), send_sem.at[k - 1], recv_sem.at[k - 1], (g, y_peer(k))) for k in range(1, SIDE)
        ]

    def to_sides(src_of, dst_of, send_sem, recv_sem):
        return [
            send(src_of(side), dst_of(side), send_sem.at[side], recv_sem.at[side], (g, leaf_peer(k)))
            for side, k in ((0, 1), (1, N_LEAF - 1))
        ]

    def eight(i):
        return pl.ds(pl.multiple_of(i * 8, 8), 8)

    def edge(side):
        return pl.ds((LD - 2) * LEAF if side == 0 else 0, 2 * LEAF)

    x_pts = to_x(px.at[x], px.at[x], xs1, xr1)
    halo_live = to_sides(lambda side: lt, lambda side: hl.at[side], hs1, hr1)
    halo_pts = to_sides(lambda side: pts.at[:, edge(side)], lambda side: hp.at[side], hs2, hr2)
    y_pts = to_y(lambda k: ty.at[y], lambda k: ty.at[y], ys1, yr1)

    for load in loads[1:]:
        load.wait()
    wr[...] = jnp.zeros((256, 256), f32)

    def up(t, carry):
        rows = pl.ds(pl.multiple_of(t * LEAF, LEAF), LEAF)
        r = jnp.concatenate(split(rh[rows, :]), axis=1)
        R[pl.ds(pl.multiple_of((t + NEAR) * LEAF, LEAF), LEAF), :] = r
        basis = jnp.concatenate(split(lb[rows, :]), axis=1)
        inner = nb[pl.ds(pl.multiple_of(t * RANK, RANK), RANK), :]
        inner_row = jnp.concatenate(split(inner), axis=1)
        w = halves(dot(basis, jnp.concatenate([inner_row, inner_row], axis=0)))
        WW[rows, :] = jnp.concatenate(split(w), axis=1)
        high, low = split(inner.T)
        flat_w = lax.dot_general(
            jnp.concatenate([jnp.concatenate([high, high], axis=1), jnp.concatenate([low, low], axis=1)], axis=0),
            basis, NT, preferred_element_type=f32,
        )
        wr[...] += dot(jnp.concatenate(split(flat_w[:128] + flat_w[128:]), axis=0), r)
        return carry

    lax.fori_loop(0, LD, up, 0)
    node_coef = halves(wr[0:128, :] + wr[128:256, :])
    ctp[...] = mm3(node_coef.T, gb[...])
    sum_coef = to_leaf(lambda p: ctp.at[eight(p)], lambda k: gcs.at[k - 1], s1, r1)
    src_c[x] = node_coef
    for copy in x_pts:
        copy.wait_recv()
    gpy[...] = px[0, D:, :] + px[1, D:, :] + px[2, D:, :] + px[3, D:, :]
    y_sum = to_y(lambda k: gpy, lambda k: py.at[k - 1], ys2, yr2)
    x_coef = to_x(src_c.at[x], src_c.at[x], xs3, xr3)
    halo_rhs = to_sides(lambda side: rh.at[edge(side)], lambda side: hr.at[side], hs3, hr3)

    diagonal = rows_of((LEAF, LEAF)) == lax.broadcasted_iota(jnp.int32, (LEAF, LEAF), 1)
    eye = diagonal.astype(f32).astype(bf16)

    def own_features(t, carry):
        cols = pl.ds(pl.multiple_of(t * LEAF, LEAF), LEAF)
        u, v = features(pts[:, cols], column(bias[0], t), one_hot(t + NEAR))
        U[cols, :] = flip(u, eye)
        VT[:, pl.ds(pl.multiple_of(t * LEAF + PAD, LEAF), LEAF)] = v
        return carry

    lax.fori_loop(0, LD, own_features, 0)

    def add_tiles(u_ref, u_row, out_ref, count, s, depth):
        rows = pl.ds(u_row, count * LEAF)
        source = pl.ds(pl.multiple_of((s + NEAR) * LEAF, LEAF), depth * LEAF)
        k_high, k_low = kernel_block(u_ref[rows, :], VT[:, source])
        out_ref[rows, :] += apply_block(k_high, k_low, R[source, :])

    def tiles(t, count, s, depth):
        add_tiles(U, pl.multiple_of(t * LEAF, LEAF), acc, count, s, depth)

    def inner_block(b):
        tiles(b * 4, 4, b * 4 - 2, 8)

    def outer_block(i, carry):
        tiles(i * 12, 4, i * 10, 6)
        return carry

    def corners(j, carry):
        tiles(j * 4 + 4, 2, j * 4, 2)
        tiles(j * 4 + 2, 2, j * 4 + 6, 2)
        return carry

    acc[...] = jnp.zeros((ROWS, NRHS), f32)

    for copy in halo_live + halo_pts:
        copy.wait_recv()
    bias[1] = mask_table(hl[0], -N_LEAF)
    bias[2] = mask_table(hl[1], N_LEAF)
    for side in range(2):
        for i in range(2):
            cols = slice(i * LEAF, (i + 1) * LEAF)
            t = i + LD - 2 if side == 0 else i
            s = i - 2 if side == 0 else i + LD
            u, v = features(hp[side, :, cols], column(bias[1 + side], t), one_hot(s + NEAR))
            UH[side, cols, :] = flip(u, eye)
            VT[:, pl.ds((s + NEAR) * LEAF, LEAF)] = v
    accH[...] = jnp.zeros((2, 2 * LEAF, NRHS), f32)
    add_tiles(UH.at[1], 0, accH.at[1], 2, LD - 4, 4)
    add_tiles(UH.at[0], 0, accH.at[0], 2, 2, 2)
    halo_part = to_sides(lambda side: accH.at[1 - side], lambda side: hpart.at[side], hs4, hr4)

    inner_block(1)

    for copy in y_sum:
        copy.wait_recv()
    gall[g] = gpy[...] + py[0] + py[1] + py[2]
    all_pts = to_grp(gall.at[g], gall.at[g], gs1, gr1)
    for copy in sum_coef:
        copy.wait_recv()
    total = ctp[eight(l), :]
    for k in range(N_LEAF - 1):
        total = total + gcs[k]
    fmine[...] = total
    gc_out = to_grp(fmine, gc.at[g], gs2, gr2)
    gc[g] = jnp.zeros((8, 128), f32)

    for copy in y_pts + x_coef:
        copy.wait_recv()
    us, vs, rs = [], [], []
    for i in range(SIDE):
        u_col = base_u()
        for j in range(SIDE):
            close = jnp.abs(SIDE * x + i - SIDE * j - y) < 2
            u_col = u_col + jnp.where(rows_of((D, 1)) == MASK + j, jnp.where(close, DEAD, 0.0), 0.0)
        us.append(features(ty[i], u_col, None)[0].T)
        vs.append(features(px[i, 0:D, :], None, one_hot(i))[1])
        rs.append(jnp.concatenate(split(src_c[i]), axis=1))
    k_high, k_low = kernel_block(jnp.concatenate(us, axis=0), jnp.concatenate(vs, axis=1))
    field = apply_block(k_high, k_low, jnp.concatenate(rs, axis=0))
    for i in range(SIDE):
        part[i] = field[i * 128 : (i + 1) * 128]
    y_field = to_y(lambda k: part.at[lax.rem(y + k, SIDE)], lambda k: fr.at[k - 1], ys4, yr4)

    inner_block(2)

    for copy in gc_out + all_pts:
        copy.wait_recv()
    u_own = features(gall[g], base_u(), None)[0].T
    v_all = jnp.concatenate([features(gall[h], None, base_v())[1] for h in range(N_GRP)], axis=1)
    k_high, k_low = kernel_block(u_own, v_all)
    columns = jnp.concatenate([gc[h] for h in range(N_GRP)], axis=1)
    c_high = columns.astype(bf16).astype(f32)
    both = jnp.concatenate([c_high, columns - c_high], axis=0).astype(bf16)
    mine = lax.dot_general(both, k_high, NT, preferred_element_type=f32)
    mine += lax.dot_general(both, k_low, NT, preferred_element_type=f32)
    ft[eight(l), :] = mine[0:8] + mine[8:16]
    field_out = to_leaf(lambda p: ft.at[eight(l)], lambda k: ft.at[eight(l)], s2, r2)

    lax.fori_loop(0, 2, outer_block, 0)
    lax.fori_loop(0, 3, corners, 0)

    for side in range(2):
        halo_rhs[side].wait_recv()
        s = -2 if side == 0 else LD
        for i in range(2):
            r = jnp.concatenate(split(hr[side, i * LEAF : (i + 1) * LEAF, :]), axis=1)
            R[pl.ds((s + i + NEAR) * LEAF, LEAF), :] = r
    tiles(2, 2, -2, 2)
    tiles(12, 4, LD, 2)
    for copy in halo_part:
        copy.wait_recv()
    acc[edge(1), :] += hpart[0]
    acc[edge(0), :] += hpart[1]

    for copy in y_field + field_out:
        copy.wait_recv()
    node_field = part[y] + fr[0] + fr[1] + fr[2] + mm3(gb[...], ft[...].T)
    row = jnp.concatenate(split(node_field), axis=1)
    both = jnp.concatenate([row, row], axis=0)
    stores = []
    for i in range(4):
        rows = pl.ds(i * 1024, 1024)
        acc[rows, :] += halves(dot(WW[rows, :], both))
        store = pltpu.make_async_copy(acc.at[rows], out.at[rows], out_sem.at[i])
        store.start()
        stores.append(store)
    for copy in sends:
        copy.wait_send()
    for store in stores:
        store.wait()


def per_device(
    points, rhs, leaf_basis, leaf_skeleton, node_basis, node_skeleton, group_basis, group_skeleton, near_live
):
    any_ = pl.BlockSpec(memory_space=pl.ANY)
    vmem = pl.BlockSpec(memory_space=pltpu.VMEM)
    V = pltpu.VMEM
    ext = ROWS + 2 * PAD
    scratch = [
        V((D, ROWS), f32), V((ROWS, NRHS), f32), V((ROWS, RANK), f32), V((LD * RANK, RANK), f32), V((RANK, RANK), f32),
        V((ROWS, 256), bf16), V((256, ext), bf16), V((ext, 256), bf16), V((ROWS, 256), bf16), V((ROWS, NRHS), f32),
        V((3, D, 128), f32), V((256, 256), f32), V((16, 128), f32), V((128, 128), f32),
        V((SIDE, 2 * D, 128), f32), V((SIDE, D, 128), f32), V((D, 128), f32), V((SIDE - 1, D, 128), f32),
        V((N_GRP, D, 128), f32), V((128, 128), f32), V((SIDE, 128, 128), f32), V((128, 128), f32),
        V((N_LEAF - 1, 8, 128), f32), V((N_GRP, 8, 128), f32), V((8, 128), f32), V((128, 128), f32),
        V((SIDE, 128, 128), f32), V((SIDE - 1, 128, 128), f32),
        V((2, D, 2 * LEAF), f32), V((2, 16, 128), f32), V((2, 2 * LEAF, NRHS), f32), V((2, 2 * LEAF, 256), bf16),
        V((2, 2 * LEAF, NRHS), f32), V((2, 2 * LEAF, NRHS), f32),
    ]
    counts = (5, 4, 3, 3, 3, 3, 3, 3, 3, 3, 3, 3, 7, 7, 7, 7, 15, 15, 15, 15, 2, 2, 2, 2, 2, 2, 2, 2)
    scratch += [pltpu.SemaphoreType.DMA((n,)) for n in counts]
    return pl.pallas_call(
        body,
        out_shape=jax.ShapeDtypeStruct((ROWS, NRHS), f32),
        in_specs=[any_] * 5 + [vmem] * 4,
        out_specs=any_,
        scratch_shapes=scratch,
        compiler_params=pltpu.CompilerParams(
            collective_id=0, has_side_effects=True, vmem_limit_bytes=56 * 1024 * 1024
        ),
    )(
        points.T, rhs, leaf_basis.reshape(ROWS, RANK), node_basis.reshape(LD * RANK, RANK),
        group_basis.reshape(RANK, RANK), leaf_skeleton, node_skeleton, group_skeleton, near_live,
    )


def solution(mesh):
    return jax.shard_map(
        per_device,
        mesh=mesh,
        in_specs=(
            P(("grp", "leaf"), None),
            P(("grp", "leaf"), None),
            P(("grp", "leaf"), None, None),
            P(("grp", "leaf"), None),
            P(("grp", "leaf"), None, None),
            P(("grp", "leaf"), None),
            P("grp", "leaf", None),
            P("grp", None),
            P(("grp", "leaf"), None),
        ),
        out_specs=P(("grp", "leaf"), None),
        check_vma=False,
    )
```

```python
import functools
import math

import jax
import jax.numpy as jnp
from jax import lax
from jax.experimental import pallas as pl
from jax.experimental.pallas import tpu as pltpu
from jax.sharding import PartitionSpec as P

MESH = pl.DeviceIdType.MESH
f32 = jnp.float32
bf16 = jnp.bfloat16
NT = (((1,), (1,)), ((), ()))

D = 64
NRHS = 128
LEAF = 256
RANK = 128
NEAR = 4
LD = 16
ROWS = LD * LEAF
N_GRP = 8
N_LEAF = 16
SIDE = 4
ALPHA = math.sqrt(4.0 / D * math.log2(math.e))
DEAD = -32768.0
MASK = 8
PAD = NEAR * LEAF


def dot(a, b):
    return jnp.dot(a, b, preferred_element_type=f32)


def split(x):
    high = x.astype(bf16)
    return high, (x - high.astype(f32)).astype(bf16)


def pieces(x):
    high = x.astype(bf16)
    rest = x - high.astype(f32)
    middle = rest.astype(bf16)
    return jnp.concatenate([high, middle, (rest - middle.astype(f32)).astype(bf16)], axis=0)


def thirds(x):
    n = x.shape[0] // 3
    return x[:n] + x[n : 2 * n] + x[2 * n :]


def halves(x):
    return x[:, :128] + x[:, 128:]


def mm3(a, b):
    a_high, a_low = split(a)
    b_high, b_low = split(b)
    row = jnp.concatenate([b_high, b_low], axis=1)
    return halves(dot(jnp.concatenate([a_high, a_low], axis=1), jnp.concatenate([row, row], axis=0)))


def rows_of(shape):
    return lax.broadcasted_iota(jnp.int32, shape, 0)


def base_u():
    row = rows_of((D, 1))
    return ((row >= 3) & (row < 6)).astype(f32)


def base_v():
    return (rows_of((D, 1)) < 3).astype(f32)


def one_hot(s):
    return base_v() + (rows_of((D, 1)) == MASK + s).astype(f32)


def features(coordinates, u_col, v_col):
    n = coordinates.shape[1]
    scaled = coordinates * ALPHA
    high = scaled.astype(bf16)
    low = (scaled - high.astype(f32)).astype(bf16)
    both = high.astype(f32) + low.astype(f32)
    norm = -0.5 * jnp.sum(both * both, axis=0, keepdims=True)
    n1 = norm.astype(bf16).astype(f32)
    n2 = (norm - n1).astype(bf16).astype(f32)
    n3 = norm - n1 - n2
    row = rows_of((8, n))
    result = []
    for first, col, blocks in ((0, u_col, (high, low, high)), (3, v_col, (high, high, low))):
        if col is None:
            result.append(None)
            continue
        top = jnp.where(
            row == first, n1, jnp.where(row == first + 1, n2, jnp.where(row == first + 2, n3, col[:8]))
        )
        extra = jnp.concatenate([top, jnp.broadcast_to(col[8:], (D - 8, n))], axis=0).astype(bf16)
        result.append(jnp.concatenate([*blocks, extra], axis=0))
    return result


def flip(x, eye):
    return lax.dot_general(eye, x, NT, preferred_element_type=f32).astype(bf16)


def kernel_block(u, v):
    return split(jnp.exp2(dot(u, v)))


def apply_block(k_high, k_low, r):
    return halves(dot(k_high, r)) + dot(k_low, r[:, :128])


def mask_table(alive, shift):
    shape = (D, 128)
    row = rows_of(shape)
    leaf = lax.broadcasted_iota(jnp.int32, shape, 1)
    table = jnp.where((row >= MASK) & (row < MASK + LD + 2 * NEAR), DEAD, 0.0)
    for j in range(2 * NEAR + 1):
        here = (row == leaf + (MASK + j + shift)) & (row >= MASK)
        table = jnp.where(here, (1.0 - alive[j : j + 1, :]) * DEAD, table)
    return table + base_u()


def column(table, t):
    lane = lax.broadcasted_iota(jnp.int32, table.shape, 1)
    return jnp.sum(jnp.where(lane == t, table, 0.0), axis=1, keepdims=True)


def body(
    points, rhs, leaf_basis, node_basis, group_basis, leaf_skel, node_skel, group_skel, live,
    out,
    pts, rh, lb, nb, gb, U, VT, R, WW, acc, bias, wr, lt, flat,
    px, ty, gpy, py, gall, coef, src_c, ctp, gcs, gc, fmine, ft, part, fr,
    hp, hl, hr, UH, accH, hpart,
    in_sem, out_sem, xs1, xr1, ys1, yr1, ys2, yr2, xs3, xr3, ys4, yr4,
    gs1, gr1, gs2, gr2, s1, r1, s2, r2, hs1, hr1, hs2, hr2, hs3, hr3, hs4, hr4,
):
    g = lax.axis_index("grp")
    l = lax.axis_index("leaf")
    x = l // SIDE
    y = lax.rem(l, SIDE)

    def leaf_peer(k):
        return lax.rem(l + k, N_LEAF)

    def grp_peer(k):
        return lax.rem(g + k, N_GRP)

    def x_peer(k):
        return lax.rem(x + k, SIDE) * SIDE + y

    def y_peer(k):
        return x * SIDE + lax.rem(y + k, SIDE)

    barrier = pltpu.get_barrier_semaphore()
    for k in range(1, N_LEAF):
        pl.semaphore_signal(barrier, inc=1, device_id=(g, leaf_peer(k)), device_id_type=MESH)
    for k in range(1, N_GRP):
        pl.semaphore_signal(barrier, inc=1, device_id=(grp_peer(k), l), device_id_type=MESH)

    loads = [
        pltpu.make_async_copy(src, dst, in_sem.at[i])
        for i, (src, dst) in enumerate(
            ((points, pts), (rhs, rh), (node_basis, nb), (leaf_basis, lb), (group_basis, gb))
        )
    ]
    for load in loads:
        load.start()

    flat[...] = jnp.zeros((128, 128), f32)
    flat[0:LD, 0 : 2 * NEAR + 1] = live[...].astype(f32)
    alive = flat[...].T[0:16]
    lt[...] = alive
    bias[0] = mask_table(alive, 0)

    skeleton = node_skel[...]
    leaf = skeleton // RANK
    place = lax.rem(skeleton, RANK)
    hot = (rows_of((RANK, RANK)) == place).astype(bf16)
    table = dot(leaf_skel[...].astype(f32).astype(bf16), hot)
    within = jnp.sum(jnp.where(rows_of((LD, RANK)) == leaf, table, 0.0), axis=0, keepdims=True)
    target = leaf.astype(f32) * LEAF + within
    row256 = rows_of((LEAF, RANK)).astype(f32)
    loads[0].wait()

    def pick(t, total):
        hot = (row256 == target - t.astype(f32) * LEAF).astype(bf16)
        cols = pl.ds(pl.multiple_of(t * LEAF, LEAF), LEAF)
        return total + dot(pieces(pts[:, cols]), hot)

    node_pts = thirds(lax.fori_loop(0, LD, pick, jnp.zeros((3 * D, RANK), f32), unroll=4))
    hot = (rows_of((RANK, RANK)) + l * RANK == group_skel[...]).astype(bf16)
    px[x, 0:D, :] = node_pts
    px[x, D : 2 * D, :] = thirds(dot(pieces(node_pts), hot))
    ty[y] = node_pts

    diagonal = rows_of((LEAF, LEAF)) == lax.broadcasted_iota(jnp.int32, (LEAF, LEAF), 1)
    eye = diagonal.astype(f32).astype(bf16)

    def own_features(t, carry):
        cols = pl.ds(pl.multiple_of(t * LEAF, LEAF), LEAF)
        u, v = features(pts[:, cols], column(bias[0], t), one_hot(t + NEAR))
        U[cols, :] = flip(u, eye)
        VT[:, pl.ds(pl.multiple_of(t * LEAF + PAD, LEAF), LEAF)] = v
        return carry


    for load in loads[1:]:
        load.wait()
    wr[...] = jnp.zeros((256, 256), f32)

    def up(t, carry):
        rows = pl.ds(pl.multiple_of(t * LEAF, LEAF), LEAF)
        r = jnp.concatenate(split(rh[rows, :]), axis=1)
        R[pl.ds(pl.multiple_of((t + NEAR) * LEAF, LEAF), LEAF), :] = r
        basis = jnp.concatenate(split(lb[rows, :]), axis=1)
        inner = nb[pl.ds(pl.multiple_of(t * RANK, RANK), RANK), :]
        inner_row = jnp.concatenate(split(inner), axis=1)
        w = halves(dot(basis, jnp.concatenate([inner_row, inner_row], axis=0)))
        WW[rows, :] = jnp.concatenate(split(w), axis=1)
        high, low = split(inner.T)
        flat_w = lax.dot_general(
            jnp.concatenate([jnp.concatenate([high, high], axis=1), jnp.concatenate([low, low], axis=1)], axis=0),
            basis, NT, preferred_element_type=f32,
        )
        wr[...] += dot(jnp.concatenate(split(flat_w[:128] + flat_w[128:]), axis=0), r)
        return carry

    lax.fori_loop(0, LD // 2, up, 0, unroll=4)
    pl.semaphore_wait(barrier, N_LEAF + N_GRP - 2)

    sends = []

    def send(src, dst, send_sem, recv_sem, device):
        copy = pltpu.make_async_remote_copy(
            src_ref=src, dst_ref=dst, send_sem=send_sem, recv_sem=recv_sem, device_id=device, device_id_type=MESH
        )
        copy.start()
        sends.append(copy)
        return copy

    def to_leaf(src_of, dst_of, send_sem, recv_sem):
        return [
            send(src_of(leaf_peer(k)), dst_of(k), send_sem.at[k - 1], recv_sem.at[k - 1], (g, leaf_peer(k)))
            for k in range(1, N_LEAF)
        ]

    def to_grp(src, dst, send_sem, recv_sem):
        return [
            send(src, dst, send_sem.at[k - 1], recv_sem.at[k - 1], (grp_peer(k), l)) for k in range(1, N_GRP)
        ]

    def to_x(src, dst, send_sem, recv_sem, others):
        result, beside = [], []
        for k in (1, 3, 2):
            result.append(send(src, dst, send_sem.at[k - 1], recv_sem.at[k - 1], (g, x_peer(k))))
            if others:
                beside.append(others.pop(0)())
        beside += [other() for other in others]
        return result, beside

    def to_y(src_of, dst_of, send_sem, recv_sem):
        return [
            send(src_of(k), dst_of(k), send_sem.at[k - 1], recv_sem.at[k - 1], (g, y_peer(k))) for k in (1, 3, 2)
        ]

    def to_sides(src_of, dst_of, send_sem, recv_sem):
        return [
            functools.partial(
                send, src_of(side), dst_of(side), send_sem.at[side], recv_sem.at[side], (g, leaf_peer(k))
            )
            for side, k in ((0, 1), (1, N_LEAF - 1))
        ]

    def eight(i):
        return pl.ds(pl.multiple_of(i * 8, 8), 8)

    def edge(side):
        return pl.ds((LD - 2) * LEAF if side == 0 else 0, 2 * LEAF)

    def send_rhs(i):
        def rows(side):
            return pl.ds(((LD - 2 if side == 0 else 0) + i) * LEAF, LEAF)

        return to_sides(
            lambda side: rhs.at[rows(side)], lambda side: hr.at[side, pl.ds(i * LEAF, LEAF)], hs3.at[i], hr3.at[i]
        )

    x_pts, _ = to_x(px.at[x], px.at[x], xs1, xr1, [])
    y_pts = to_y(lambda k: ty.at[y], lambda k: ty.at[y], ys1, yr1)
    lax.fori_loop(LD // 2, LD, up, 0, unroll=4)
    node_coef = halves(wr[0:128, :] + wr[128:256, :])
    ctp[...] = mm3(node_coef.T, gb[...])
    sum_coef = to_leaf(lambda p: ctp.at[eight(p)], lambda k: gcs.at[k - 1], s1, r1)
    src_c[x] = node_coef
    halo_pts = to_sides(lambda side: pts.at[:, edge(side)], lambda side: hp.at[side], hs2, hr2)
    halo_live = to_sides(lambda side: lt, lambda side: hl.at[side], hs1, hr1)
    x_coef, halo_pts = to_x(src_c.at[x], src_c.at[x], xs3, xr3, halo_pts + halo_live)
    lax.fori_loop(0, LD, own_features, 0, unroll=4)

    def add_tiles(u_ref, u_row, out_ref, count, s, depth):
        rows = pl.ds(u_row, count * LEAF)
        source = pl.ds(pl.multiple_of((s + NEAR) * LEAF, LEAF), depth * LEAF)
        k_high, k_low = kernel_block(u_ref[rows, :], VT[:, source])
        out_ref[rows, :] += apply_block(k_high, k_low, R[source, :])

    def tiles(t, count, s, depth):
        add_tiles(U, pl.multiple_of(t * LEAF, LEAF), acc, count, s, depth)

    def inner_block(b):
        tiles(b * 4, 4, b * 4 - 2, 8)

    def outer_block(i, carry):
        tiles(i * 12, 4, i * 10, 6)
        return carry

    def corners(j, carry):
        tiles(j * 4 + 4, 2, j * 4, 2)
        tiles(j * 4 + 2, 2, j * 4 + 6, 2)
        return carry

    acc[...] = jnp.zeros((ROWS, NRHS), f32)

    lax.fori_loop(0, 1, outer_block, 0)
    for copy in x_pts:
        copy.wait_recv()
    gpy[...] = px[0, D:, :] + px[1, D:, :] + px[2, D:, :] + px[3, D:, :]
    y_sum = to_y(lambda k: gpy, lambda k: py.at[k - 1], ys2, yr2)
    halo_rhs = [start() for start in send_rhs(1)]
    inner_block(1)

    for copy in y_sum:
        copy.wait_recv()
    gall[g] = gpy[...] + py[0] + py[1] + py[2]
    all_pts = to_grp(gall.at[g], gall.at[g], gs1, gr1)
    for copy in sum_coef:
        copy.wait_recv()
    total = ctp[eight(l), :]
    for k in range(N_LEAF - 1):
        total = total + gcs[k]
    fmine[...] = total
    gc_out = to_grp(fmine, gc.at[g], gs2, gr2)
    gc[g] = jnp.zeros((8, 128), f32)

    halo_rhs += [start() for start in send_rhs(0)]

    for copy in halo_pts:
        copy.wait_recv()
    bias[1] = mask_table(hl[0], -N_LEAF)
    bias[2] = mask_table(hl[1], N_LEAF)
    for side in range(2):
        for i in range(2):
            cols = slice(i * LEAF, (i + 1) * LEAF)
            t = i + LD - 2 if side == 0 else i
            s = i - 2 if side == 0 else i + LD
            u, v = features(hp[side, :, cols], column(bias[1 + side], t), one_hot(s + NEAR))
            UH[side, cols, :] = flip(u, eye)
            VT[:, pl.ds((s + NEAR) * LEAF, LEAF)] = v
    accH[...] = jnp.zeros((2, 2 * LEAF, NRHS), f32)
    add_tiles(UH.at[1], 0, accH.at[1], 2, LD - 4, 4)
    add_tiles(UH.at[0], 0, accH.at[0], 2, 2, 2)
    def send_part(i):
        rows = pl.ds(i * LEAF, LEAF)
        return [
            start()
            for start in to_sides(
                lambda side: accH.at[1 - side, rows], lambda side: hpart.at[side, rows], hs4.at[i], hr4.at[i]
            )
        ]

    halo_part = send_part(0)

    for copy in y_pts + x_coef:
        copy.wait_recv()
    us, vs, rs = [], [], []
    for i in range(SIDE):
        u_col = base_u()
        for j in range(SIDE):
            close = jnp.abs(SIDE * x + i - SIDE * j - y) < 2
            u_col = u_col + jnp.where(rows_of((D, 1)) == MASK + j, jnp.where(close, DEAD, 0.0), 0.0)
        us.append(features(ty[i], u_col, None)[0].T)
        vs.append(features(px[i, 0:D, :], None, one_hot(i))[1])
        rs.append(jnp.concatenate(split(src_c[i]), axis=1))
    k_high, k_low = kernel_block(jnp.concatenate(us, axis=0), jnp.concatenate(vs, axis=1))
    field = apply_block(k_high, k_low, jnp.concatenate(rs, axis=0))
    for i in range(SIDE):
        part[i] = field[i * 128 : (i + 1) * 128]
    inner_block(2)

    for copy in gc_out + all_pts:
        copy.wait_recv()
    u_own = features(gall[g], base_u(), None)[0].T
    v_all = jnp.concatenate([features(gall[h], None, base_v())[1] for h in range(N_GRP)], axis=1)
    k_high, k_low = kernel_block(u_own, v_all)
    columns = jnp.concatenate([gc[h] for h in range(N_GRP)], axis=1)
    c_high = columns.astype(bf16).astype(f32)
    both = jnp.concatenate([c_high, columns - c_high], axis=0).astype(bf16)
    mine = lax.dot_general(both, k_high, NT, preferred_element_type=f32)
    mine += lax.dot_general(both, k_low, NT, preferred_element_type=f32)
    ft[eight(l), :] = mine[0:8] + mine[8:16]
    field_out = to_leaf(lambda p: ft.at[eight(l)], lambda k: ft.at[eight(l)], s2, r2)

    y_field = to_y(lambda k: part.at[lax.rem(y + k, SIDE)], lambda k: fr.at[k - 1], ys4, yr4)
    halo_part += send_part(1)

    lax.fori_loop(1, 2, outer_block, 0)
    lax.fori_loop(0, 3, corners, 0, unroll=3)

    for copy in halo_rhs:
        copy.wait_recv()
    for side in range(2):
        s = -2 if side == 0 else LD
        for i in range(2):
            r = jnp.concatenate(split(hr[side, i * LEAF : (i + 1) * LEAF, :]), axis=1)
            R[pl.ds((s + i + NEAR) * LEAF, LEAF), :] = r
    tiles(2, 2, -2, 2)
    tiles(12, 4, LD, 2)
    for copy in halo_part:
        copy.wait_recv()
    acc[edge(1), :] += hpart[0]
    acc[edge(0), :] += hpart[1]

    for copy in y_field + field_out:
        copy.wait_recv()
    node_field = part[y] + fr[0] + fr[1] + fr[2] + mm3(gb[...], ft[...].T)
    row = jnp.concatenate(split(node_field), axis=1)
    both = jnp.concatenate([row, row], axis=0)
    stores = []
    for i in range(4):
        rows = pl.ds(i * 1024, 1024)
        acc[rows, :] += halves(dot(WW[rows, :], both))
        store = pltpu.make_async_copy(acc.at[rows], out.at[rows], out_sem.at[i])
        store.start()
        stores.append(store)
    for copy in sends:
        copy.wait_send()
    for store in stores:
        store.wait()


def per_device(
    points, rhs, leaf_basis, leaf_skeleton, node_basis, node_skeleton, group_basis, group_skeleton, near_live
):
    any_ = pl.BlockSpec(memory_space=pl.ANY)
    vmem = pl.BlockSpec(memory_space=pltpu.VMEM)
    V = pltpu.VMEM
    ext = ROWS + 2 * PAD
    scratch = [
        V((D, ROWS), f32), V((ROWS, NRHS), f32), V((ROWS, RANK), f32), V((LD * RANK, RANK), f32), V((RANK, RANK), f32),
        V((ROWS, 256), bf16), V((256, ext), bf16), V((ext, 256), bf16), V((ROWS, 256), bf16), V((ROWS, NRHS), f32),
        V((3, D, 128), f32), V((256, 256), f32), V((16, 128), f32), V((128, 128), f32),
        V((SIDE, 2 * D, 128), f32), V((SIDE, D, 128), f32), V((D, 128), f32), V((SIDE - 1, D, 128), f32),
        V((N_GRP, D, 128), f32), V((128, 128), f32), V((SIDE, 128, 128), f32), V((128, 128), f32),
        V((N_LEAF - 1, 8, 128), f32), V((N_GRP, 8, 128), f32), V((8, 128), f32), V((128, 128), f32),
        V((SIDE, 128, 128), f32), V((SIDE - 1, 128, 128), f32),
        V((2, D, 2 * LEAF), f32), V((2, 16, 128), f32), V((2, 2 * LEAF, NRHS), f32), V((2, 2 * LEAF, 256), bf16),
        V((2, 2 * LEAF, NRHS), f32), V((2, 2 * LEAF, NRHS), f32),
    ]
    counts = (5, 4, 3, 3, 3, 3, 3, 3, 3, 3, 3, 3, 7, 7, 7, 7, 15, 15, 15, 15, 2, 2, 2, 2, (2, 2), (2, 2), (2, 2), (2, 2))
    scratch += [pltpu.SemaphoreType.DMA(n if isinstance(n, tuple) else (n,)) for n in counts]
    return pl.pallas_call(
        body,
        out_shape=jax.ShapeDtypeStruct((ROWS, NRHS), f32),
        in_specs=[any_] * 5 + [vmem] * 4,
        out_specs=any_,
        scratch_shapes=scratch,
        compiler_params=pltpu.CompilerParams(
            collective_id=0, has_side_effects=True, vmem_limit_bytes=56 * 1024 * 1024
        ),
    )(
        points.T, rhs, leaf_basis.reshape(ROWS, RANK), node_basis.reshape(LD * RANK, RANK),
        group_basis.reshape(RANK, RANK), leaf_skeleton, node_skeleton, group_skeleton, near_live,
    )


def solution(mesh):
    return jax.shard_map(
        per_device,
        mesh=mesh,
        in_specs=(
            P(("grp", "leaf"), None),
            P(("grp", "leaf"), None),
            P(("grp", "leaf"), None, None),
            P(("grp", "leaf"), None),
            P(("grp", "leaf"), None, None),
            P(("grp", "leaf"), None),
            P("grp", "leaf", None),
            P("grp", None),
            P(("grp", "leaf"), None),
        ),
        out_specs=P(("grp", "leaf"), None),
        check_vma=False,
    )
```

```python
import functools
import math

import jax
import jax.numpy as jnp
from jax import lax
from jax.experimental import pallas as pl
from jax.experimental.pallas import tpu as pltpu
from jax.sharding import PartitionSpec as P

MESH = pl.DeviceIdType.MESH
f32 = jnp.float32
bf16 = jnp.bfloat16
NT = (((1,), (1,)), ((), ()))

D = 64
NRHS = 128
LEAF = 256
RANK = 128
NEAR = 4
LD = 16
ROWS = LD * LEAF
N_GRP = 8
N_LEAF = 16
SIDE = 4
ALPHA = math.sqrt(4.0 / D * math.log2(math.e))
DEAD = -32768.0
MASK = 8
PAD = NEAR * LEAF


def dot(a, b):
    return jnp.dot(a, b, preferred_element_type=f32)


def split(x):
    high = x.astype(bf16)
    return high, (x - high.astype(f32)).astype(bf16)


def pieces(x):
    high = x.astype(bf16)
    rest = x - high.astype(f32)
    middle = rest.astype(bf16)
    return jnp.concatenate([high, middle, (rest - middle.astype(f32)).astype(bf16)], axis=0)


def thirds(x):
    n = x.shape[0] // 3
    return x[:n] + x[n : 2 * n] + x[2 * n :]


def halves(x):
    return x[:, :128] + x[:, 128:]


def mm3(a, b):
    a_high, a_low = split(a)
    b_high, b_low = split(b)
    row = jnp.concatenate([b_high, b_low], axis=1)
    return halves(dot(jnp.concatenate([a_high, a_low], axis=1), jnp.concatenate([row, row], axis=0)))


def rows_of(shape):
    return lax.broadcasted_iota(jnp.int32, shape, 0)


def base_u():
    row = rows_of((D, 1))
    return ((row >= 3) & (row < 6)).astype(f32)


def base_v():
    return (rows_of((D, 1)) < 3).astype(f32)


def one_hot(s):
    return base_v() + (rows_of((D, 1)) == MASK + s).astype(f32)


def features(coordinates, u_col, v_col):
    n = coordinates.shape[1]
    scaled = coordinates * ALPHA
    high = scaled.astype(bf16)
    low = (scaled - high.astype(f32)).astype(bf16)
    both = high.astype(f32) + low.astype(f32)
    norm = -0.5 * jnp.sum(both * both, axis=0, keepdims=True)
    n1 = norm.astype(bf16).astype(f32)
    n2 = (norm - n1).astype(bf16).astype(f32)
    n3 = norm - n1 - n2
    row = rows_of((8, n))
    result = []
    for first, col, blocks in ((0, u_col, (high, low, high)), (3, v_col, (high, high, low))):
        if col is None:
            result.append(None)
            continue
        top = jnp.where(
            row == first, n1, jnp.where(row == first + 1, n2, jnp.where(row == first + 2, n3, col[:8]))
        )
        extra = jnp.concatenate([top, jnp.broadcast_to(col[8:], (D - 8, n))], axis=0).astype(bf16)
        result.append(jnp.concatenate([*blocks, extra], axis=0))
    return result


def flip(x, eye):
    return lax.dot_general(eye, x, NT, preferred_element_type=f32).astype(bf16)


def kernel_block(u, v):
    return split(jnp.exp2(dot(u, v)))


def apply_block(k_high, k_low, r):
    return halves(dot(k_high, r)) + dot(k_low, r[:, :128])


def mask_table(alive, shift):
    shape = (D, 128)
    row = rows_of(shape)
    leaf = lax.broadcasted_iota(jnp.int32, shape, 1)
    table = jnp.where((row >= MASK) & (row < MASK + LD + 2 * NEAR), DEAD, 0.0)
    for j in range(2 * NEAR + 1):
        here = (row == leaf + (MASK + j + shift)) & (row >= MASK)
        table = jnp.where(here, (1.0 - alive[j : j + 1, :]) * DEAD, table)
    return table + base_u()


def column(table, t):
    lane = lax.broadcasted_iota(jnp.int32, table.shape, 1)
    return jnp.sum(jnp.where(lane == t, table, 0.0), axis=1, keepdims=True)


def body(
    points, rhs, leaf_basis, node_basis, group_basis, leaf_skel, node_skel, group_skel, live,
    out,
    pts, rh, lb, nb, gb, U, VT, R, WW, acc, bias, wr, lt, flat,
    px, ty, gpy, py, gall, coef, src_c, ctp, gcs, gc, fmine, ft, part, fr,
    hp, hl, hr, UH, accH, hpart,
    in_sem, out_sem, xs1, xr1, ys1, yr1, ys2, yr2, xs3, xr3, ys4, yr4,
    gs1, gr1, gs2, gr2, s1, r1, s2, r2, hs1, hr1, hs2, hr2, hs3, hr3, hs4, hr4,
):
    g = lax.axis_index("grp")
    l = lax.axis_index("leaf")
    x = l // SIDE
    y = lax.rem(l, SIDE)

    def leaf_peer(k):
        return lax.rem(l + k, N_LEAF)

    def grp_peer(k):
        return lax.rem(g + k, N_GRP)

    def x_peer(k):
        return lax.rem(x + k, SIDE) * SIDE + y

    def y_peer(k):
        return x * SIDE + lax.rem(y + k, SIDE)

    barrier = pltpu.get_barrier_semaphore()
    for k in range(1, N_LEAF):
        pl.semaphore_signal(barrier, inc=1, device_id=(g, leaf_peer(k)), device_id_type=MESH)
    for k in range(1, N_GRP):
        pl.semaphore_signal(barrier, inc=1, device_id=(grp_peer(k), l), device_id_type=MESH)

    loads = [
        pltpu.make_async_copy(src, dst, in_sem.at[i])
        for i, (src, dst) in enumerate(
            ((points, pts), (rhs, rh), (node_basis, nb), (leaf_basis, lb), (group_basis, gb))
        )
    ]
    for load in loads:
        load.start()

    flat[...] = jnp.zeros((128, 128), f32)
    flat[0:LD, 0 : 2 * NEAR + 1] = live[...].astype(f32)
    alive = flat[...].T[0:16]
    lt[...] = alive
    bias[0] = mask_table(alive, 0)

    skeleton = node_skel[...]
    leaf = skeleton // RANK
    place = lax.rem(skeleton, RANK)
    hot = (rows_of((RANK, RANK)) == place).astype(bf16)
    table = dot(leaf_skel[...].astype(f32).astype(bf16), hot)
    within = jnp.sum(jnp.where(rows_of((LD, RANK)) == leaf, table, 0.0), axis=0, keepdims=True)
    target = leaf.astype(f32) * LEAF + within
    row256 = rows_of((LEAF, RANK)).astype(f32)
    loads[0].wait()

    def pick(t, total):
        hot = (row256 == target - t.astype(f32) * LEAF).astype(bf16)
        cols = pl.ds(pl.multiple_of(t * LEAF, LEAF), LEAF)
        return total + dot(pieces(pts[:, cols]), hot)

    node_pts = thirds(lax.fori_loop(0, LD, pick, jnp.zeros((3 * D, RANK), f32), unroll=4))
    hot = (rows_of((RANK, RANK)) + l * RANK == group_skel[...]).astype(bf16)
    px[x, 0:D, :] = node_pts
    px[x, D : 2 * D, :] = thirds(dot(pieces(node_pts), hot))
    ty[y] = node_pts

    diagonal = rows_of((LEAF, LEAF)) == lax.broadcasted_iota(jnp.int32, (LEAF, LEAF), 1)
    eye = diagonal.astype(f32).astype(bf16)

    def own_features(t, carry):
        cols = pl.ds(pl.multiple_of(t * LEAF, LEAF), LEAF)
        u, v = features(pts[:, cols], column(bias[0], t), one_hot(t + NEAR))
        U[cols, :] = flip(u, eye)
        VT[:, pl.ds(pl.multiple_of(t * LEAF + PAD, LEAF), LEAF)] = v
        return carry


    for load in loads[1:]:
        load.wait()
    wr[...] = jnp.zeros((256, 256), f32)

    def up(t, carry):
        rows = pl.ds(pl.multiple_of(t * LEAF, LEAF), LEAF)
        r = jnp.concatenate(split(rh[rows, :]), axis=1)
        R[pl.ds(pl.multiple_of((t + NEAR) * LEAF, LEAF), LEAF), :] = r
        basis = jnp.concatenate(split(lb[rows, :]), axis=1)
        inner = nb[pl.ds(pl.multiple_of(t * RANK, RANK), RANK), :]
        inner_row = jnp.concatenate(split(inner), axis=1)
        w = halves(dot(basis, jnp.concatenate([inner_row, inner_row], axis=0)))
        WW[rows, :] = jnp.concatenate(split(w), axis=1)
        high, low = split(inner.T)
        flat_w = lax.dot_general(
            jnp.concatenate([jnp.concatenate([high, high], axis=1), jnp.concatenate([low, low], axis=1)], axis=0),
            basis, NT, preferred_element_type=f32,
        )
        wr[...] += dot(jnp.concatenate(split(flat_w[:128] + flat_w[128:]), axis=0), r)
        return carry

    lax.fori_loop(0, LD // 2, up, 0, unroll=4)
    pl.semaphore_wait(barrier, N_LEAF + N_GRP - 2)

    sends = []

    def send(src, dst, send_sem, recv_sem, device):
        copy = pltpu.make_async_remote_copy(
            src_ref=src, dst_ref=dst, send_sem=send_sem, recv_sem=recv_sem, device_id=device, device_id_type=MESH
        )
        copy.start()
        sends.append(copy)
        return copy

    def to_leaf(src_of, dst_of, send_sem, recv_sem):
        return [
            send(src_of(leaf_peer(k)), dst_of(k), send_sem.at[k - 1], recv_sem.at[k - 1], (g, leaf_peer(k)))
            for k in range(1, N_LEAF)
        ]

    def to_grp(src, dst, send_sem, recv_sem):
        return [
            send(src, dst, send_sem.at[k - 1], recv_sem.at[k - 1], (grp_peer(k), l)) for k in range(1, N_GRP)
        ]

    def to_x(src, dst, send_sem, recv_sem, others):
        result, beside = [], []
        for k in (1, 3, 2):
            result.append(send(src, dst, send_sem.at[k - 1], recv_sem.at[k - 1], (g, x_peer(k))))
            if others:
                beside.append(others.pop(0)())
        beside += [other() for other in others]
        return result, beside

    def to_y(src_of, dst_of, send_sem, recv_sem):
        return [
            send(src_of(k), dst_of(k), send_sem.at[k - 1], recv_sem.at[k - 1], (g, y_peer(k))) for k in (1, 3, 2)
        ]

    def to_sides(src_of, dst_of, send_sem, recv_sem):
        return [
            functools.partial(
                send, src_of(side), dst_of(side), send_sem.at[side], recv_sem.at[side], (g, leaf_peer(k))
            )
            for side, k in ((0, 1), (1, N_LEAF - 1))
        ]

    def eight(i):
        return pl.ds(pl.multiple_of(i * 8, 8), 8)

    def edge(side):
        return pl.ds((LD - 2) * LEAF if side == 0 else 0, 2 * LEAF)

    def send_rhs(i):
        def rows(side):
            return pl.ds(((LD - 2 if side == 0 else 0) + i) * LEAF, LEAF)

        return to_sides(
            lambda side: rhs.at[rows(side)], lambda side: hr.at[side, pl.ds(i * LEAF, LEAF)], hs3.at[i], hr3.at[i]
        )

    x_pts, _ = to_x(px.at[x], px.at[x], xs1, xr1, [])
    y_pts = to_y(lambda k: ty.at[y], lambda k: ty.at[y], ys1, yr1)
    lax.fori_loop(LD // 2, LD, up, 0, unroll=4)
    node_coef = halves(wr[0:128, :] + wr[128:256, :])
    ctp[...] = mm3(node_coef.T, gb[...])
    sum_coef = to_leaf(lambda p: ctp.at[eight(p)], lambda k: gcs.at[k - 1], s1, r1)
    src_c[x] = node_coef
    halo_pts = to_sides(lambda side: pts.at[:, edge(side)], lambda side: hp.at[side], hs2, hr2)
    halo_live = to_sides(lambda side: lt, lambda side: hl.at[side], hs1, hr1)
    x_coef, halo_pts = to_x(src_c.at[x], src_c.at[x], xs3, xr3, halo_pts + halo_live)
    lax.fori_loop(0, LD, own_features, 0, unroll=4)

    def add_tiles(u_ref, u_row, out_ref, count, s, depth):
        rows = pl.ds(u_row, count * LEAF)
        source = pl.ds(pl.multiple_of((s + NEAR) * LEAF, LEAF), depth * LEAF)
        k_high, k_low = kernel_block(u_ref[rows, :], VT[:, source])
        out_ref[rows, :] += apply_block(k_high, k_low, R[source, :])

    def tiles(t, count, s, depth):
        add_tiles(U, pl.multiple_of(t * LEAF, LEAF), acc, count, s, depth)

    def inner_block(b):
        tiles(b * 4, 4, b * 4 - 2, 8)

    def outer_block(i, carry):
        tiles(i * 12, 4, i * 10, 6)
        return carry

    def corners(j, carry):
        tiles(j * 4 + 4, 2, j * 4, 2)
        tiles(j * 4 + 2, 2, j * 4 + 6, 2)
        return carry

    acc[...] = jnp.zeros((ROWS, NRHS), f32)

    lax.fori_loop(0, 1, outer_block, 0)
    for copy in x_pts:
        copy.wait_recv()
    gpy[...] = px[0, D:, :] + px[1, D:, :] + px[2, D:, :] + px[3, D:, :]
    y_sum = to_y(lambda k: gpy, lambda k: py.at[k - 1], ys2, yr2)
    halo_rhs = [start() for start in send_rhs(1)]
    inner_block(1)

    for copy in y_sum:
        copy.wait_recv()
    gall[g] = gpy[...] + py[0] + py[1] + py[2]
    all_pts = to_grp(gall.at[g], gall.at[g], gs1, gr1)
    for copy in sum_coef:
        copy.wait_recv()
    total = ctp[eight(l), :]
    for k in range(N_LEAF - 1):
        total = total + gcs[k]
    fmine[...] = total
    gc_out = to_grp(fmine, gc.at[g], gs2, gr2)
    gc[g] = jnp.zeros((8, 128), f32)

    halo_rhs += [start() for start in send_rhs(0)]

    for copy in halo_pts:
        copy.wait_recv()
    bias[1] = mask_table(hl[0], -N_LEAF)
    bias[2] = mask_table(hl[1], N_LEAF)
    for side in range(2):
        for i in range(2):
            cols = slice(i * LEAF, (i + 1) * LEAF)
            t = i + LD - 2 if side == 0 else i
            s = i - 2 if side == 0 else i + LD
            u, v = features(hp[side, :, cols], column(bias[1 + side], t), one_hot(s + NEAR))
            UH[side, cols, :] = flip(u, eye)
            VT[:, pl.ds((s + NEAR) * LEAF, LEAF)] = v
    accH[...] = jnp.zeros((2, 2 * LEAF, NRHS), f32)
    add_tiles(UH.at[1], 0, accH.at[1], 2, LD - 4, 4)
    add_tiles(UH.at[0], 0, accH.at[0], 2, 2, 2)
    def send_part(i):
        rows = pl.ds(i * LEAF, LEAF)
        return [
            start()
            for start in to_sides(
                lambda side: accH.at[1 - side, rows], lambda side: hpart.at[side, rows], hs4.at[i], hr4.at[i]
            )
        ]

    halo_part = send_part(0)

    for copy in y_pts + x_coef:
        copy.wait_recv()
    us, vs, rs = [], [], []
    for i in range(SIDE):
        u_col = base_u()
        for j in range(SIDE):
            close = jnp.abs(SIDE * x + i - SIDE * j - y) < 2
            u_col = u_col + jnp.where(rows_of((D, 1)) == MASK + j, jnp.where(close, DEAD, 0.0), 0.0)
        us.append(features(ty[i], u_col, None)[0].T)
        vs.append(features(px[i, 0:D, :], None, one_hot(i))[1])
        rs.append(jnp.concatenate(split(src_c[i]), axis=1))
    k_high, k_low = kernel_block(jnp.concatenate(us, axis=0), jnp.concatenate(vs, axis=1))
    field = apply_block(k_high, k_low, jnp.concatenate(rs, axis=0))
    for i in range(SIDE):
        part[i] = field[i * 128 : (i + 1) * 128]
    y_field = to_y(lambda k: part.at[lax.rem(y + k, SIDE)], lambda k: fr.at[k - 1], ys4, yr4)
    inner_block(2)

    for copy in gc_out + all_pts:
        copy.wait_recv()
    u_own = features(gall[g], base_u(), None)[0].T
    v_all = jnp.concatenate([features(gall[h], None, base_v())[1] for h in range(N_GRP)], axis=1)
    k_high, k_low = kernel_block(u_own, v_all)
    columns = jnp.concatenate([gc[h] for h in range(N_GRP)], axis=1)
    c_high = columns.astype(bf16).astype(f32)
    both = jnp.concatenate([c_high, columns - c_high], axis=0).astype(bf16)
    mine = lax.dot_general(both, k_high, NT, preferred_element_type=f32)
    mine += lax.dot_general(both, k_low, NT, preferred_element_type=f32)
    ft[eight(l), :] = mine[0:8] + mine[8:16]
    field_out = to_leaf(lambda p: ft.at[eight(l)], lambda k: ft.at[eight(l)], s2, r2)

    halo_part += send_part(1)

    lax.fori_loop(1, 2, outer_block, 0)
    lax.fori_loop(0, 3, corners, 0, unroll=3)

    for copy in halo_rhs:
        copy.wait_recv()
    for side in range(2):
        s = -2 if side == 0 else LD
        for i in range(2):
            r = jnp.concatenate(split(hr[side, i * LEAF : (i + 1) * LEAF, :]), axis=1)
            R[pl.ds((s + i + NEAR) * LEAF, LEAF), :] = r
    tiles(2, 2, -2, 2)
    tiles(12, 4, LD, 2)
    for copy in halo_part:
        copy.wait_recv()
    acc[edge(1), :] += hpart[0]
    acc[edge(0), :] += hpart[1]

    for copy in y_field + field_out:
        copy.wait_recv()
    node_field = part[y] + fr[0] + fr[1] + fr[2] + mm3(gb[...], ft[...].T)
    row = jnp.concatenate(split(node_field), axis=1)
    both = jnp.concatenate([row, row], axis=0)
    stores = []
    for i in range(4):
        rows = pl.ds(i * 1024, 1024)
        acc[rows, :] += halves(dot(WW[rows, :], both))
        store = pltpu.make_async_copy(acc.at[rows], out.at[rows], out_sem.at[i])
        store.start()
        stores.append(store)
    for copy in sends:
        copy.wait_send()
    for store in stores:
        store.wait()


def per_device(
    points, rhs, leaf_basis, leaf_skeleton, node_basis, node_skeleton, group_basis, group_skeleton, near_live
):
    any_ = pl.BlockSpec(memory_space=pl.ANY)
    vmem = pl.BlockSpec(memory_space=pltpu.VMEM)
    V = pltpu.VMEM
    ext = ROWS + 2 * PAD
    scratch = [
        V((D, ROWS), f32), V((ROWS, NRHS), f32), V((ROWS, RANK), f32), V((LD * RANK, RANK), f32), V((RANK, RANK), f32),
        V((ROWS, 256), bf16), V((256, ext), bf16), V((ext, 256), bf16), V((ROWS, 256), bf16), V((ROWS, NRHS), f32),
        V((3, D, 128), f32), V((256, 256), f32), V((16, 128), f32), V((128, 128), f32),
        V((SIDE, 2 * D, 128), f32), V((SIDE, D, 128), f32), V((D, 128), f32), V((SIDE - 1, D, 128), f32),
        V((N_GRP, D, 128), f32), V((128, 128), f32), V((SIDE, 128, 128), f32), V((128, 128), f32),
        V((N_LEAF - 1, 8, 128), f32), V((N_GRP, 8, 128), f32), V((8, 128), f32), V((128, 128), f32),
        V((SIDE, 128, 128), f32), V((SIDE - 1, 128, 128), f32),
        V((2, D, 2 * LEAF), f32), V((2, 16, 128), f32), V((2, 2 * LEAF, NRHS), f32), V((2, 2 * LEAF, 256), bf16),
        V((2, 2 * LEAF, NRHS), f32), V((2, 2 * LEAF, NRHS), f32),
    ]
    counts = (5, 4, 3, 3, 3, 3, 3, 3, 3, 3, 3, 3, 7, 7, 7, 7, 15, 15, 15, 15, 2, 2, 2, 2, (2, 2), (2, 2), (2, 2), (2, 2))
    scratch += [pltpu.SemaphoreType.DMA(n if isinstance(n, tuple) else (n,)) for n in counts]
    return pl.pallas_call(
        body,
        out_shape=jax.ShapeDtypeStruct((ROWS, NRHS), f32),
        in_specs=[any_] * 5 + [vmem] * 4,
        out_specs=any_,
        scratch_shapes=scratch,
        compiler_params=pltpu.CompilerParams(
            collective_id=0, has_side_effects=True, vmem_limit_bytes=56 * 1024 * 1024
        ),
    )(
        points.T, rhs, leaf_basis.reshape(ROWS, RANK), node_basis.reshape(LD * RANK, RANK),
        group_basis.reshape(RANK, RANK), leaf_skeleton, node_skeleton, group_skeleton, near_live,
    )


def solution(mesh):
    return jax.shard_map(
        per_device,
        mesh=mesh,
        in_specs=(
            P(("grp", "leaf"), None),
            P(("grp", "leaf"), None),
            P(("grp", "leaf"), None, None),
            P(("grp", "leaf"), None),
            P(("grp", "leaf"), None, None),
            P(("grp", "leaf"), None),
            P("grp", "leaf", None),
            P("grp", None),
            P(("grp", "leaf"), None),
        ),
        out_specs=P(("grp", "leaf"), None),
        check_vma=False,
    )
```
